32 devices in a mesh: seq: 8 (over z, x), ctx: 4 (over y, core).
Axes of the slice: x: 2, y: 2, z: 4, core: 2. Of those that a mesh axis runs over, the one named last changes fastest.
Arguments:
- tokens: bfloat16 [8, 2048, 1088], P('seq', 'ctx'), may hold values from -6 to 6
- segments: int32 [8, 2048], P('seq', 'ctx'), may hold values from 0 to 4, as said below
- cotangent: bfloat16 [8, 2048, 1088], P('seq', 'ctx'), may hold values from -6 to 6
- gain_one: float32 [1088], replicated, may hold values from 0.5 to 1.5
- shift_one: float32 [1088], replicated, may hold values from -3 to 3
- w_qkv: bfloat16 [1088, 3264], P('seq', 'ctx'), may hold values from -0.25 to 0.25
- bias_q: float32 [1088], replicated, may hold values from -3 to 3
- bias_v: float32 [1088], replicated, may hold values from -3 to 3
- w_out: bfloat16 [1088, 1088], P('seq', 'ctx'), may hold values from -1.5 to 1.5
- bias_out: float32 [1088], replicated, may hold values from -3 to 3
- gain_two: float32 [1088], replicated, may hold values from 0.5 to 1.5
- shift_two: float32 [1088], replicated, may hold values from -3 to 3
- w_up: bfloat16 [1088, 4352], P('seq', 'ctx'), may hold values from -0.1875 to 0.1875
- bias_up: float32 [4352], replicated, may hold values from -3 to 3
- w_down: bfloat16 [4352, 1088], P('seq', 'ctx'), may hold values from -0.09375 to 0.09375
- bias_down: float32 [1088], replicated, may hold values from -3 to 3
Outputs:
- output: bfloat16 [8, 2048, 1088], P('seq', 'ctx')
- grad_tokens: float32 [8, 2048, 1088], P('seq', 'ctx')
- grad_gain_one: float32 [1088], replicated
- grad_shift_one: float32 [1088], replicated
- grad_w_qkv: float32 [1088, 3264], P('seq', 'ctx')
- grad_bias_q: float32 [1088], replicated
- grad_bias_v: float32 [1088], replicated
- grad_w_out: float32 [1088, 1088], P('seq', 'ctx')
- grad_bias_out: float32 [1088], replicated
- grad_gain_two: float32 [1088], replicated
- grad_shift_two: float32 [1088], replicated
- grad_w_up: float32 [1088, 4352], P('seq', 'ctx')
- grad_bias_up: float32 [4352], replicated
- grad_w_down: float32 [4352, 1088], P('seq', 'ctx')
- grad_bias_down: float32 [1088], replicated
The draws below stay inside these ranges and needn't reach their ends.
Inputs may be any that keep to these rules, and one draw needn't show every extreme that they name: `segments`: in each sequence the numbers start at 0, never fall and rise by at most one from a position to the next; each sequence holds exactly five documents. Its third document begins among the first 512 positions and ends among the last 512; the short documents before and after it are pieces that packing cut at the sequence's edges.
All inputs are finite; a program needn't handle non-finite values.
Results may differ from the reference program's by a relative error of at most 0.018.
Values may be sent and summed in bfloat16 or wider, within the bound.
No kernel may reach another device: no remote copies, remote signals or barrier semaphores. Data moves between devices by JAX's collectives and lax.ppermute only.
A program may use at most 192 MiB of HBM per device.

```python
import jax
import jax.numpy as jnp
from jax import lax

HEADS = 17
HEAD_DIM = 64
FF = 4352
SEQ_LEN = 2048
D = 1088
SEQUENCES = 8
TOK_DEV = 512


def draw_segments(key, part):
    key = jax.random.fold_in(key, 11)
    key_first, key_last, key_early, key_late = jax.random.split(key, 4)
    first = jax.random.randint(key_first, (SEQUENCES, 1), 2, TOK_DEV)
    last = jax.random.randint(key_last, (SEQUENCES, 1), SEQ_LEN - TOK_DEV + 1, SEQ_LEN - 1)
    early = jax.random.randint(key_early, (SEQUENCES, 1), 1, first)
    late = jax.random.randint(key_late, (SEQUENCES, 1), last + 1, SEQ_LEN)
    position = jnp.arange(SEQ_LEN, dtype=jnp.int32)[None, :]
    starts = (position == early) | (position == first) | (position == last) | (position == late)
    return jnp.cumsum(starts.astype(jnp.int32), axis=1).astype(jnp.int32)


def block_scale(key, extent, cuts, low, largest):
    factor_of, own = 1.0, jax.random.fold_in(key, 6)
    for dim, blocks in cuts:
        draws = jnp.exp(jax.random.uniform(jax.random.fold_in(own, dim), (blocks,), jnp.float32, low / len(cuts), largest / len(cuts)))
        factor_of = factor_of * jnp.repeat(draws, extent[dim] // blocks).reshape([-1 if axis == dim else 1 for axis in range(len(extent))])
    return factor_of


def scatter_about(stream_key, extent, deviation, reach, cuts=(), kind=jnp.bfloat16):
    values = deviation * jax.random.normal(stream_key, extent, jnp.float32)
    if cuts:
        values = values * block_scale(stream_key, extent, cuts, -0.22, 0.18)
    return jnp.clip(values, -reach, reach).astype(kind)


def setup_inputs(seed: int = 0) -> dict:
    key_list = jax.random.split(jax.random.key(seed), 17)
    return {
        "tokens": scatter_about(key_list[0], (SEQUENCES, SEQ_LEN, D), 1.0, 6.0, ((0, 8), (1, 4))),
        "segments": draw_segments(jax.random.fold_in(key_list[16], 71), 0),
        "cotangent": scatter_about(key_list[2], (SEQUENCES, SEQ_LEN, D), 1.0, 6.0, ((0, 8), (1, 4))),
        "gain_one": jnp.clip(1.0 + 0.1 * jax.random.normal(key_list[3], (D,), jnp.float32), 0.5, 1.5),
        "shift_one": scatter_about(key_list[4], (D,), 0.3, 3.0, (), jnp.float32),
        "w_qkv": scatter_about(key_list[5], (D, 3 * D), (D // 2) ** -0.5, 0.25, ((0, 8), (1, 4))),
        "bias_q": scatter_about(key_list[6], (D,), 0.3, 3.0, (), jnp.float32),
        "bias_v": scatter_about(key_list[7], (D,), 0.3, 3.0, (), jnp.float32),
        "w_out": scatter_about(key_list[8], (D, D), (D // 64) ** -0.5, 1.5, ((0, 8), (1, 4))),
        "bias_out": scatter_about(key_list[9], (D,), 0.3, 3.0, (), jnp.float32),
        "gain_two": jnp.clip(1.0 + 0.1 * jax.random.normal(key_list[10], (D,), jnp.float32), 0.5, 1.5),
        "shift_two": scatter_about(key_list[11], (D,), 0.3, 3.0, (), jnp.float32),
        "w_up": scatter_about(key_list[12], (D, FF), D ** -0.5, 0.1875, ((0, 8), (1, 4))),
        "bias_up": scatter_about(key_list[13], (FF,), 0.5, 3.0, (), jnp.float32),
        "w_down": scatter_about(key_list[14], (FF, D), FF ** -0.5, 0.09375, ((0, 8), (1, 4))),
        "bias_down": scatter_about(key_list[15], (D,), 0.3, 3.0, (), jnp.float32),
    }


@jax.custom_vjp
def low(v):
    return lax.optimization_barrier(v.astype(jnp.bfloat16)).astype(jnp.float32)

@jax.custom_vjp
def low_back(v):
    return v

def low_keep(v):
    return (low(v), None)

def low_pass(kept, grad):
    return (grad,)

def back_keep(v):
    return (v, None)

def back_low(kept, grad):
    return (low(grad),)
low.defvjp(low_keep, low_pass)
low_back.defvjp(back_keep, back_low)
highest = lax.Precision.HIGHEST
eps = 1e-05
neg_big = -1e+30

def layer_norm(values, norm_gain, norm_shift):
    average = lax.optimization_barrier(jnp.mean(values, axis=-1, keepdims=True))
    centred = values - average
    variance = lax.optimization_barrier(jnp.mean(centred * centred, axis=-1, keepdims=True))
    return centred * lax.rsqrt(variance + eps) * norm_gain + norm_shift

def attend(queries, keys, values, segment):
    length = queries.shape[0]
    query_heads = queries.reshape(length, HEADS, HEAD_DIM)
    key_heads = keys.reshape(length, HEADS, HEAD_DIM)
    value_heads = values.reshape(length, HEADS, HEAD_DIM)
    scores = jnp.einsum('qhd,khd->hqk', query_heads, key_heads, precision=highest) * HEAD_DIM ** (-0.5)
    scores = low_back(scores)
    position = jnp.arange(length, dtype=jnp.int32)
    allowed = (position[None, :] <= position[:, None]) & (segment[None, :] == segment[:, None])
    scores = jnp.where(allowed[None], scores, neg_big)
    soft = low(jax.nn.softmax(scores, axis=-1))
    result = jnp.einsum('hqk,khd->qhd', soft, value_heads, precision=highest)
    return result.reshape(length, HEADS * HEAD_DIM)

def layer(params, inputs, segment):
    gain_one, shift_one, w_qkv, bias_q, bias_v, w_out, bias_out, gain_two, shift_two, w_up, bias_up, w_down, bias_down = params
    model_width = HEADS * HEAD_DIM
    normed_one = low(layer_norm(inputs, gain_one, shift_one))
    projected = jnp.dot(normed_one, w_qkv, precision=highest)
    queries = low(low_back(projected[:, :model_width] + bias_q))
    keys = low(low_back(projected[:, model_width:2 * model_width]))
    values = low(low_back(projected[:, 2 * model_width:] + bias_v))
    attended = low(low_back(attend(queries, keys, values, segment)))
    branch = low_back(jnp.dot(attended, w_out, precision=highest) + bias_out)
    middle = inputs + branch
    normed_two = low(layer_norm(middle, gain_two, shift_two))
    hidden_pre = low_back(jnp.dot(normed_two, w_up, precision=highest) + bias_up)
    activated = low(jax.nn.gelu(hidden_pre, approximate=False))
    mlp_out = low_back(jnp.dot(activated, w_down, precision=highest) + bias_down)
    return middle + mlp_out

def reference(tokens, segments, cotangent, gain_one, shift_one, w_qkv, bias_q, bias_v, w_out, bias_out, gain_two, shift_two, w_up, bias_up, w_down, bias_down):
    params = tuple((member.astype(jnp.float32) for member in (gain_one, shift_one, w_qkv, bias_q, bias_v, w_out, bias_out, gain_two, shift_two, w_up, bias_up, w_down, bias_down)))
    inputs = tokens.astype(jnp.float32)

    def forward(inputs_all, params_all):

        def single(paired):
            return layer(params_all, paired[0], paired[1])
        return lax.map(jax.checkpoint(single), (inputs_all, segments))
    result, pullback = jax.vjp(forward, inputs, params)
    grad_inputs, grads = pullback(cotangent.astype(jnp.float32))
    return (result.astype(jnp.bfloat16), grad_inputs, grads[0], grads[1], grads[2], grads[3], grads[4], grads[5], grads[6], grads[7], grads[8], grads[9], grads[10], grads[11], grads[12])
```

```python
import functools

import jax
import jax.numpy as jnp
from jax import lax
from jax.experimental import pallas as pl
from jax.experimental.pallas import tpu as pltpu
from jax.sharding import PartitionSpec as P

HEADS = 17
HEAD_DIM = 64

eps = 1e-05
neg_big = -1e30
f32 = jnp.float32
bf16 = jnp.bfloat16

NN = (((1,), (0,)), ((), ()))
NT = (((1,), (1,)), ((), ()))
TN = (((0,), (0,)), ((), ()))


def mm(left, right, dims=NN):
    return lax.dot_general(left, right, dims, preferred_element_type=f32)


def layer_norm(values, norm_gain, norm_shift):
    average = jnp.mean(values, axis=-1, keepdims=True)
    centred = values - average
    variance = jnp.mean(centred * centred, axis=-1, keepdims=True)
    return centred * lax.rsqrt(variance + eps) * norm_gain + norm_shift


def after(value, *earlier):
    return lax.optimization_barrier((value, *earlier))[0]


def allowed_tile(start, i, j, block):
    key_pos = j * block + lax.broadcasted_iota(jnp.int32, (block, block), 0)
    allowed = key_pos >= start
    if i == j:
        query_pos = i * block + lax.broadcasted_iota(jnp.int32, (block, block), 1)
        allowed = allowed & (key_pos <= query_pos)
    return allowed


def attend_kernel(block, blocks, own_ref, start_ref, qkv_ref, out_ref, log_ref):
    slots = [own_ref[0] ^ i for i in range(blocks)]
    cols = [pl.ds(pl.multiple_of(slot * block, block), block) for slot in slots]
    scale = jnp.asarray(HEAD_DIM ** (-0.5), bf16)
    for i in range(blocks):
        query = qkv_ref[0, :, cols[i]] * scale
        start = start_ref[:, cols[i]]
        scores = []
        for j in range(i + 1):
            score = mm(qkv_ref[1, :, cols[j]], query, TN)
            scores.append(jnp.where(allowed_tile(start, i, j, block), score, neg_big))
        top = functools.reduce(
            jnp.maximum, [jnp.max(score, axis=0, keepdims=True) for score in scores]
        )
        total, sums = jnp.zeros_like(top), None
        for j in range(i + 1):
            power = jnp.exp(scores[j] - top)
            total = total + jnp.sum(power, axis=0, keepdims=True)
            part = mm(qkv_ref[2, :, cols[j]], power.astype(bf16))
            sums = part if sums is None else sums + part
        out_ref[slots[i]] = (sums / total).astype(bf16)
        log_ref[0, :, cols[i]] = top + jnp.log(total)


def attend_back_kernel(
    block, blocks, own_ref, start_ref, qkv_ref, out_ref, grad_ref, log_ref, *rest
):
    back_ref, query_sum = rest[-2:]
    slots = [own_ref[0] ^ i for i in range(blocks)]
    cols = [pl.ds(pl.multiple_of(slot * block, block), block) for slot in slots]
    scale = jnp.asarray(HEAD_DIM ** (-0.5), bf16)
    dots = [
        jnp.sum(out_ref[slot].astype(f32) * grad_ref[slot].astype(f32), axis=0, keepdims=True)
        for slot in slots
    ]
    for j in range(blocks):
        key = qkv_ref[1, :, cols[j]]
        value = qkv_ref[2, :, cols[j]]
        key_sum = value_sum = None
        for i in range(j, blocks):
            query = qkv_ref[0, :, cols[i]] * scale
            grad = grad_ref[slots[i]]
            score = mm(key, query, TN)
            allowed = allowed_tile(start_ref[:, cols[i]], i, j, block)
            soft = jnp.where(allowed, jnp.exp(score - log_ref[0, :, cols[i]]), 0.0)
            back = (soft * (mm(value, grad, TN) - dots[i])).astype(bf16)
            value_part = mm(grad, soft.astype(bf16), NT)
            key_part = mm(query, back, NT)
            value_sum = value_part if value_sum is None else value_sum + value_part
            key_sum = key_part if key_sum is None else key_sum + key_part
            if j == 0:
                query_sum[i] = mm(key, back)
            else:
                query_sum[i] += mm(key, back)
        back_ref[1, :, cols[j]] = key_sum.astype(bf16)
        back_ref[2, :, cols[j]] = value_sum.astype(bf16)
    for i in range(blocks):
        back_ref[0, :, cols[i]] = (query_sum[i] * HEAD_DIM ** (-0.5)).astype(bf16)


def attend(own, start, qkv, block, first, count):
    _, width, length = qkv.shape
    blocks = length // block
    pairs = count * block * block * blocks * (blocks + 1) // 2
    return pl.pallas_call(
        functools.partial(attend_kernel, block, blocks),
        grid_spec=pltpu.PrefetchScalarGridSpec(
            num_scalar_prefetch=1,
            grid=(count,),
            in_specs=[
                pl.BlockSpec((1, length), lambda h, own: (0, 0)),
                pl.BlockSpec((3, HEAD_DIM, length), lambda h, own: (0, first + h, 0)),
            ],
            out_specs=[
                pl.BlockSpec((blocks, HEAD_DIM, block), lambda h, own: (0, h, 0)),
                pl.BlockSpec((1, 1, length), lambda h, own: (h, 0, 0)),
            ],
        ),
        out_shape=[
            jax.ShapeDtypeStruct((blocks, count * HEAD_DIM, block), bf16),
            jax.ShapeDtypeStruct((count, 1, length), f32),
        ],
        compiler_params=pltpu.CompilerParams(vmem_limit_bytes=40 * 2**20),
        cost_estimate=pl.CostEstimate(
            flops=pairs * 4 * 256 * 2,
            bytes_accessed=count * HEAD_DIM * length * 8,
            transcendentals=pairs,
        ),
        name="attend",
    )(own, start, qkv)


def attend_back(own, start, qkv, out, grad, log, block, first, count, held):
    _, width, length = qkv.shape
    blocks = length // block
    pairs = count * block * block * blocks * (blocks + 1) // 2
    tile = pl.BlockSpec((3, HEAD_DIM, length), lambda h, own: (0, first + h, 0))
    side = pl.BlockSpec((blocks, HEAD_DIM, block), lambda h, own: (0, h, 0))
    in_specs = [
        pl.BlockSpec((1, length), lambda h, own: (0, 0)),
        tile,
        side,
        side,
        pl.BlockSpec((1, 1, length), lambda h, own: (h, 0, 0)),
    ]
    operands = (own, start, qkv, out, grad, log)
    aliases = {}
    if held is not None:
        in_specs.append(pl.BlockSpec(memory_space=pl.ANY))
        operands = (*operands, held)
        aliases = {len(operands) - 1: 0}
    return pl.pallas_call(
        functools.partial(attend_back_kernel, block, blocks),
        grid_spec=pltpu.PrefetchScalarGridSpec(
            num_scalar_prefetch=1,
            grid=(count,),
            in_specs=in_specs,
            out_specs=tile,
            scratch_shapes=[pltpu.VMEM((blocks, HEAD_DIM, block), f32)],
        ),
        out_shape=jax.ShapeDtypeStruct(qkv.shape, bf16),
        input_output_aliases=aliases,
        compiler_params=pltpu.CompilerParams(vmem_limit_bytes=40 * 2**20),
        cost_estimate=pl.CostEstimate(
            flops=pairs * 8 * 256 * 2,
            bytes_accessed=count * HEAD_DIM * length * 18,
            transcendentals=pairs,
        ),
        name="attend_back",
    )(*operands)


def solution(mesh):
    n_seq, n_ctx = mesh.shape["seq"], mesh.shape["ctx"]
    per_device = -(-HEADS // n_ctx)
    share = per_device * HEAD_DIM
    padded = share * n_ctx
    cycle = list(range(0, n_seq, 2)) + list(range(1, n_seq, 2))[::-1]
    place = [cycle.index(s) for s in range(n_seq)]
    ring_right = [(cycle[p], cycle[(p + 1) % n_seq]) for p in range(n_seq)]
    ring_left = [(cycle[p], cycle[(p - 1) % n_seq]) for p in range(n_seq)]
    steps_right, steps_left = n_seq // 2, (n_seq - 1) // 2
    groups = [(g, min(2, per_device - g)) for g in range(0, per_device, 2)]

    def swap(value, distance):
        return lax.ppermute(value, "ctx", [(c, c ^ distance) for c in range(n_ctx)])

    def ctx_gather(value):
        blocks = [value]
        for r in range(1, n_ctx):
            blocks.append(swap(blocks[r - 1], 1) if r % 2 else swap(value, r))
        return blocks

    def ctx_exchange(blocks):
        return [blocks[0]] + [swap(blocks[r], r) for r in range(1, n_ctx)]

    def ctx_reduce(parts):
        sums = [
            parts[r].astype(f32) + swap(parts[r + 1], 1).astype(f32) for r in range(0, n_ctx, 2)
        ]
        total = sums[0]
        for r in range(2, n_ctx, 2):
            total = total + swap(sums[r // 2].astype(bf16), r).astype(f32)
        return total

    def in_order(blocks, own, axis):
        size = blocks[0].shape[axis]
        shape = list(blocks[0].shape)
        shape[axis] = size * n_ctx
        whole = jnp.zeros(shape, blocks[0].dtype)
        for r, piece in enumerate(blocks):
            whole = lax.dynamic_update_slice_in_dim(whole, piece, (own ^ r) * size, axis)
        return whole

    def body(
        tokens,
        segments,
        cotangent,
        gain_one,
        shift_one,
        w_qkv,
        bias_q,
        bias_v,
        w_out,
        bias_out,
        gain_two,
        shift_two,
        w_up,
        bias_up,
        w_down,
        bias_down,
    ):
        rows, width = tokens.shape[1:]
        hidden = w_up.shape[1] * n_ctx
        own = lax.axis_index("ctx")
        spot = jnp.asarray(place, jnp.int32)[lax.axis_index("seq")]
        at = jnp.asarray(cycle * 3, jnp.int32)

        def seq_gather(value):
            size = value.shape[0]
            whole = jnp.zeros((size * n_seq, *value.shape[1:]), value.dtype)

            def put(whole, piece, step):
                row = at[spot + n_seq + step] * size
                return lax.dynamic_update_slice_in_dim(whole, piece, row, 0)

            whole = put(whole, value, 0)
            right = left = value
            for step in range(1, steps_right + 1):
                right = lax.ppermute(right, "seq", ring_right)
                whole = put(whole, right, -step)
                if step <= steps_left:
                    left = lax.ppermute(left, "seq", ring_left)
                    whole = put(whole, left, step)
            return whole, right

        def seq_reduce(part):
            size = part.shape[0] // n_seq

            def take(step):
                row = at[spot + n_seq + step] * size
                return lax.dynamic_slice_in_dim(part, row, size, 0)

            right, left = take(steps_right), take(-steps_left)
            for step in range(steps_right - 1, -1, -1):
                right = lax.ppermute(right, "seq", ring_right).astype(f32)
                if step:
                    right = (right + take(step).astype(f32)).astype(bf16)
            for step in range(steps_left - 1, -1, -1):
                left = lax.ppermute(left, "seq", ring_left).astype(f32)
                if step:
                    left = (left + take(-step).astype(f32)).astype(bf16)
            return right + left + take(0).astype(f32)

        def all_sum(value):
            for r in [1 << b for b in range(n_ctx.bit_length() - 1)]:
                value = value + swap(value, r)
            for r in [1 << b for b in range(n_seq.bit_length() - 1)]:
                value = value + lax.ppermute(value, "seq", [(s, s ^ r) for s in range(n_seq)])
            return value

        own_array = jnp.reshape(own, (1,)).astype(jnp.int32)
        inputs = tokens[0].astype(f32)
        upstream_low = cotangent[0]
        upstream = upstream_low.astype(f32)

        w_qkv_rows = in_order(ctx_gather(w_qkv), own, 1).reshape(-1, 3, width)
        w_qkv_rows = jnp.pad(w_qkv_rows, ((0, 0), (0, 0), (0, padded - width)))
        w_qkv_rows = lax.dynamic_slice_in_dim(w_qkv_rows, own * share, share, 2)
        w_qkv_own, last = seq_gather(w_qkv_rows.reshape(-1, 3 * share))

        normed_one, norm_back_one = jax.vjp(layer_norm, inputs, gain_one, shift_one)
        normed_one_blocks = ctx_gather(normed_one.astype(bf16))
        normed_one_all = jnp.concatenate(normed_one_blocks)
        segment_all = jnp.concatenate(ctx_gather(segments[0]))
        start = jnp.zeros_like(segment_all)
        for number in range(1, 5):
            count = jnp.sum((segment_all < number).astype(jnp.int32))
            start = jnp.where(segment_all == number, count, start)
        start = start[None]

        w_out_rows = after(in_order(ctx_gather(w_out), own, 1), last)
        w_out_all, last = seq_gather(w_out_rows)
        w_up_own, last = seq_gather(after(w_up, last))
        piece = w_down.shape[0] // n_ctx
        w_down_pieces = w_down.reshape(n_ctx, piece, -1)
        w_down_rows = in_order(
            ctx_exchange(
                [lax.dynamic_index_in_dim(w_down_pieces, own ^ r, 0, False) for r in range(n_ctx)]
            ),
            own,
            1,
        )
        spread = [(b, (b % n_seq) * n_ctx + b // n_seq) for b in range(n_seq * n_ctx)]
        w_down_rows = lax.ppermute(w_down_rows, ("seq", "ctx"), spread)
        w_down_own, last = seq_gather(after(w_down_rows, last))
        upstream_all = jnp.concatenate(ctx_gather(after(upstream_low, normed_one_blocks[-1])))

        bias_qkv = jnp.concatenate(
            [
                lax.dynamic_slice_in_dim(jnp.pad(bias, (0, padded - width)), own * share, share)
                for bias in (bias_q, jnp.zeros_like(bias_q), bias_v)
            ]
        )
        qkv = (mm(w_qkv_own, normed_one_all, (((0,), (1,)), ((), ()))) + bias_qkv[:, None]).astype(
            bf16
        )
        qkv = qkv.reshape(3, share, -1)
        outs, logs, arrived = [], [], []
        for first, count in groups:
            out, log = attend(own_array, start, qkv, rows, first, count)
            outs.append(out)
            logs.append(log)
            arrived.append(ctx_exchange([out[r] for r in range(n_ctx)]))
        attended = in_order(
            [jnp.concatenate([part[r] for part in arrived]) for r in range(n_ctx)], own, 0
        )[:width]
        middle = inputs + mm(attended, w_out_all, TN) + bias_out

        normed_two, norm_back_two = jax.vjp(layer_norm, middle, gain_two, shift_two)
        normed_two_all = jnp.concatenate(ctx_gather(normed_two.astype(bf16)))
        bias_up_own = lax.dynamic_slice_in_dim(bias_up, own * w_up.shape[1], w_up.shape[1])
        hidden_pre = mm(normed_two_all, w_up_own) + bias_up_own
        cumulative = 0.5 * (1.0 + lax.erf(hidden_pre * 0.5**0.5))
        activated = (hidden_pre * cumulative).astype(bf16)
        slope = cumulative + hidden_pre * jnp.exp(-0.5 * hidden_pre * hidden_pre) * (
            0.5 / jnp.pi
        ) ** 0.5
        slope = slope.astype(bf16)

        grad_pre = (mm(upstream_all, w_down_own, NT) * slope.astype(f32)).astype(bf16)
        grad_norm_two = ctx_reduce(
            jnp.split(mm(grad_pre, w_up_own, NT).astype(bf16), n_ctx)
        )
        grad_middle_part, grad_gain_two, grad_shift_two = norm_back_two(grad_norm_two)
        grad_middle = upstream + grad_middle_part
        part_w_down = mm(activated, upstream_all, TN).astype(bf16)
        part_w_up = mm(normed_two_all, grad_pre, TN).astype(bf16)
        grad_w_down_rows = seq_reduce(part_w_down)
        grad_w_up = seq_reduce(part_w_up)

        grad_branch = grad_middle.astype(bf16)
        grad_attended = mm(w_out_all, grad_branch, NT).astype(bf16)
        grad_attended = jnp.pad(grad_attended, ((0, padded - width), (0, 0)))
        grad_attended = grad_attended.reshape(n_ctx, share, -1)
        grad_attended = [
            lax.dynamic_index_in_dim(grad_attended, own ^ r, 0, False) for r in range(n_ctx)
        ]
        back = None
        for (first, count), out, log in zip(groups, outs, logs):
            span = slice(first * HEAD_DIM, (first + count) * HEAD_DIM)
            grad_own = jnp.stack(ctx_exchange([part[span] for part in grad_attended]))
            back = attend_back(
                own_array, start, qkv, out, grad_own, log, rows, first, count, back
            )
        part_w_out = mm(attended, grad_branch).astype(bf16)
        grad_w_out_rows = seq_reduce(part_w_out)

        mlp_out = ctx_reduce(jnp.split(mm(activated, w_down_own).astype(bf16), n_ctx))
        output = middle + mlp_out + bias_down

        grad_proj = back.reshape(3 * share, -1)
        grad_norm_one = ctx_reduce(
            jnp.split(mm(grad_proj, w_qkv_own, (((0,), (1,)), ((), ()))).astype(bf16), n_ctx)
        )
        grad_input_part, grad_gain_one, grad_shift_one = norm_back_one(grad_norm_one)
        grad_tokens = grad_middle + grad_input_part
        part_w_qkv = mm(normed_one_all, grad_proj, (((0,), (1,)), ((), ()))).astype(bf16)
        grad_w_qkv_rows = seq_reduce(part_w_qkv).astype(bf16)
        grad_w_qkv = in_order(
            ctx_gather(grad_w_qkv_rows.reshape(-1, 3, share)), own, 2
        )[:, :, :width].reshape(-1, 3 * width)
        grad_w_qkv = lax.dynamic_slice_in_dim(
            grad_w_qkv, own * w_qkv.shape[1], w_qkv.shape[1], 1
        ).astype(f32)

        column = w_out.shape[1]
        grad_w_out_blocks = [
            lax.dynamic_slice_in_dim(grad_w_out_rows.astype(bf16), (own ^ r) * column, column, 1)
            for r in range(n_ctx)
        ]
        grad_w_out = ctx_reduce(grad_w_out_blocks)
        gathered = [(b, a) for a, b in spread]
        grad_w_down_rows = lax.ppermute(grad_w_down_rows.astype(bf16), ("seq", "ctx"), gathered)
        column = w_down.shape[1]
        grad_w_down = in_order(
            ctx_exchange(
                [
                    lax.dynamic_slice_in_dim(grad_w_down_rows, (own ^ r) * column, column, 1)
                    for r in range(n_ctx)
                ]
            ),
            own,
            0,
        ).astype(f32)

        grad_bias_up_own = jnp.sum(grad_pre.astype(f32), axis=0)
        early = all_sum(
            jnp.concatenate(
                [
                    jnp.sum(upstream, axis=0),
                    grad_gain_two,
                    grad_shift_two,
                    jnp.sum(grad_branch.astype(f32), axis=0),
                    lax.dynamic_update_slice_in_dim(
                        jnp.zeros((hidden,), f32), grad_bias_up_own, own * w_up.shape[1], 0
                    ),
                ]
            )
        )
        grad_bias_down, grad_gain_two, grad_shift_two, grad_bias_out = (
            early[g * width : (g + 1) * width] for g in range(4)
        )
        grad_bias_up = early[4 * width :]
        grad_bias_qkv = jnp.sum(back.astype(f32), axis=2)
        late = all_sum(
            jnp.concatenate(
                [grad_gain_one, grad_shift_one]
                + [
                    lax.dynamic_update_slice_in_dim(
                        jnp.zeros((padded,), f32), grad_bias_qkv[g], own * share, 0
                    )[:width]
                    for g in (0, 2)
                ]
            )
        )
        grad_gain_one, grad_shift_one, grad_bias_q, grad_bias_v = (
            late[g * width : (g + 1) * width] for g in range(4)
        )
        return (
            output[None].astype(bf16),
            grad_tokens[None],
            grad_gain_one,
            grad_shift_one,
            grad_w_qkv,
            grad_bias_q,
            grad_bias_v,
            grad_w_out,
            grad_bias_out,
            grad_gain_two,
            grad_shift_two,
            grad_w_up,
            grad_bias_up,
            grad_w_down,
            grad_bias_down,
        )

    block = P("seq", "ctx", None)
    split = P("seq", "ctx")
    return jax.shard_map(
        body,
        mesh=mesh,
        in_specs=(
            block,
            split,
            block,
            P(),
            P(),
            split,
            P(),
            P(),
            split,
            P(),
            P(),
            P(),
            split,
            P(),
            split,
            P(),
        ),
        out_specs=(
            block,
            block,
            P(),
            P(),
            split,
            P(),
            P(),
            split,
            P(),
            P(),
            P(),
            split,
            P(),
            split,
            P(),
        ),
        check_vma=False,
    )
```

```python
import functools

import jax
import jax.numpy as jnp
from jax import lax
from jax.experimental import pallas as pl
from jax.experimental.pallas import tpu as pltpu
from jax.sharding import PartitionSpec as P

HEADS = 17
HEAD_DIM = 64

eps = 1e-05
neg_big = -1e30
f32 = jnp.float32
bf16 = jnp.bfloat16

NN = (((1,), (0,)), ((), ()))
NT = (((1,), (1,)), ((), ()))
TN = (((0,), (0,)), ((), ()))


def mm(left, right, dims=NN):
    return lax.dot_general(left, right, dims, preferred_element_type=f32)


def layer_norm(values, norm_gain, norm_shift):
    average = jnp.mean(values, axis=-1, keepdims=True)
    centred = values - average
    variance = jnp.mean(centred * centred, axis=-1, keepdims=True)
    return centred * lax.rsqrt(variance + eps) * norm_gain + norm_shift


def after(value, *earlier):
    return lax.optimization_barrier((value, *earlier))[0]


def allowed_tile(start, i, j, block):
    key_pos = j * block + lax.broadcasted_iota(jnp.int32, (block, block), 0)
    allowed = key_pos >= start
    if i == j:
        query_pos = i * block + lax.broadcasted_iota(jnp.int32, (block, block), 1)
        allowed = allowed & (key_pos <= query_pos)
    return allowed


def attend_kernel(block, blocks, own_ref, start_ref, qkv_ref, out_ref, log_ref):
    slots = [own_ref[0] ^ i for i in range(blocks)]
    cols = [pl.ds(pl.multiple_of(slot * block, block), block) for slot in slots]
    scale = jnp.asarray(HEAD_DIM ** (-0.5), bf16)
    for i in range(blocks):
        query = qkv_ref[0, :, cols[i]] * scale
        start = start_ref[:, cols[i]]
        scores = []
        for j in range(i + 1):
            score = mm(qkv_ref[1, :, cols[j]], query, TN)
            scores.append(jnp.where(allowed_tile(start, i, j, block), score, neg_big))
        top = functools.reduce(
            jnp.maximum, [jnp.max(score, axis=0, keepdims=True) for score in scores]
        )
        total, sums = jnp.zeros_like(top), None
        for j in range(i + 1):
            power = jnp.exp(scores[j] - top)
            total = total + jnp.sum(power, axis=0, keepdims=True)
            part = mm(qkv_ref[2, :, cols[j]], power.astype(bf16))
            sums = part if sums is None else sums + part
        out_ref[slots[i]] = (sums / total).astype(bf16)
        log_ref[0, :, cols[i]] = top + jnp.log(total)


def attend_back_kernel(
    block, blocks, own_ref, start_ref, qkv_ref, out_ref, grad_ref, log_ref, *rest
):
    back_ref, query_sum = rest[-2:]
    slots = [own_ref[0] ^ i for i in range(blocks)]
    cols = [pl.ds(pl.multiple_of(slot * block, block), block) for slot in slots]
    scale = jnp.asarray(HEAD_DIM ** (-0.5), bf16)
    dots = [
        jnp.sum(out_ref[slot].astype(f32) * grad_ref[slot].astype(f32), axis=0, keepdims=True)
        for slot in slots
    ]
    for j in range(blocks):
        key = qkv_ref[1, :, cols[j]]
        value = qkv_ref[2, :, cols[j]]
        key_sum = value_sum = None
        for i in range(j, blocks):
            query = qkv_ref[0, :, cols[i]] * scale
            grad = grad_ref[slots[i]]
            score = mm(key, query, TN)
            allowed = allowed_tile(start_ref[:, cols[i]], i, j, block)
            soft = jnp.where(allowed, jnp.exp(score - log_ref[0, :, cols[i]]), 0.0)
            back = (soft * (mm(value, grad, TN) - dots[i])).astype(bf16)
            value_part = mm(grad, soft.astype(bf16), NT)
            key_part = mm(query, back, NT)
            value_sum = value_part if value_sum is None else value_sum + value_part
            key_sum = key_part if key_sum is None else key_sum + key_part
            if j == 0:
                query_sum[i] = mm(key, back)
            else:
                query_sum[i] += mm(key, back)
        back_ref[1, :, cols[j]] = key_sum.astype(bf16)
        back_ref[2, :, cols[j]] = value_sum.astype(bf16)
    for i in range(blocks):
        back_ref[0, :, cols[i]] = (query_sum[i] * HEAD_DIM ** (-0.5)).astype(bf16)


def attend(own, start, qkv, block, first, count):
    _, width, length = qkv.shape
    blocks = length // block
    pairs = count * block * block * blocks * (blocks + 1) // 2
    return pl.pallas_call(
        functools.partial(attend_kernel, block, blocks),
        grid_spec=pltpu.PrefetchScalarGridSpec(
            num_scalar_prefetch=1,
            grid=(count,),
            in_specs=[
                pl.BlockSpec((1, length), lambda h, own: (0, 0)),
                pl.BlockSpec((3, HEAD_DIM, length), lambda h, own: (0, first + h, 0)),
            ],
            out_specs=[
                pl.BlockSpec((blocks, HEAD_DIM, block), lambda h, own: (0, h, 0)),
                pl.BlockSpec((1, 1, length), lambda h, own: (h, 0, 0)),
            ],
        ),
        out_shape=[
            jax.ShapeDtypeStruct((blocks, count * HEAD_DIM, block), bf16),
            jax.ShapeDtypeStruct((count, 1, length), f32),
        ],
        compiler_params=pltpu.CompilerParams(vmem_limit_bytes=24 * 2**20),
        cost_estimate=pl.CostEstimate(
            flops=pairs * 4 * 256 * 2,
            bytes_accessed=count * HEAD_DIM * length * 8,
            transcendentals=pairs,
        ),
        name="attend",
    )(own, start, qkv)


def attend_back(own, start, qkv, out, grad, log, block, first, count, held, grad_first):
    _, width, length = qkv.shape
    blocks = length // block
    pairs = count * block * block * blocks * (blocks + 1) // 2
    tile = pl.BlockSpec((3, HEAD_DIM, length), lambda h, own: (0, first + h, 0))
    side = pl.BlockSpec((blocks, HEAD_DIM, block), lambda h, own: (0, h, 0))
    in_specs = [
        pl.BlockSpec((1, length), lambda h, own: (0, 0)),
        tile,
        side,
        pl.BlockSpec((blocks, HEAD_DIM, block), lambda h, own: (0, first - grad_first + h, 0)),
        pl.BlockSpec((1, 1, length), lambda h, own: (h, 0, 0)),
    ]
    operands = (own, start, qkv, out, grad, log)
    aliases = {}
    if held is not None:
        in_specs.append(pl.BlockSpec(memory_space=pl.ANY))
        operands = (*operands, held)
        aliases = {len(operands) - 1: 0}
    return pl.pallas_call(
        functools.partial(attend_back_kernel, block, blocks),
        grid_spec=pltpu.PrefetchScalarGridSpec(
            num_scalar_prefetch=1,
            grid=(count,),
            in_specs=in_specs,
            out_specs=tile,
            scratch_shapes=[pltpu.VMEM((blocks, HEAD_DIM, block), f32)],
        ),
        out_shape=jax.ShapeDtypeStruct(qkv.shape, bf16),
        input_output_aliases=aliases,
        compiler_params=pltpu.CompilerParams(vmem_limit_bytes=24 * 2**20),
        cost_estimate=pl.CostEstimate(
            flops=pairs * 8 * 256 * 2,
            bytes_accessed=count * HEAD_DIM * length * 18,
            transcendentals=pairs,
        ),
        name="attend_back",
    )(*operands)


def move_columns(own, sources, widths, plan, dtype):
    rows = sources[0].shape[0]

    def kernel(own_ref, *refs):
        source_refs, target_refs = refs[: len(sources)], refs[len(sources) :]
        for c, moves in enumerate(plan):

            @pl.when(own_ref[0] == c)
            def _():
                for t, (ref, width) in enumerate(zip(target_refs, widths)):
                    covered = sum(move[4] for move in moves if move[0] == t)
                    if covered < width:
                        ref[...] = jnp.zeros_like(ref)
                for t, to, s, start, count in moves:
                    piece = source_refs[s][:, start : start + count]
                    target_refs[t][:, to : to + count] = piece.astype(dtype)

    return pl.pallas_call(
        kernel,
        in_specs=[pl.BlockSpec(memory_space=pltpu.SMEM)]
        + [pl.BlockSpec(memory_space=pltpu.VMEM)] * len(sources),
        out_specs=[pl.BlockSpec(memory_space=pltpu.VMEM)] * len(widths),
        out_shape=[jax.ShapeDtypeStruct((rows, width), dtype) for width in widths],
        compiler_params=pltpu.CompilerParams(vmem_limit_bytes=32 * 2**20),
        name="move_columns",
    )(own, *sources)


def join_rows(own, blocks, dtype):
    size, width = blocks[0].shape

    def kernel(own_ref, *refs):
        for c in range(len(blocks)):

            @pl.when(own_ref[0] == c)
            def _():
                for r in range(len(blocks)):
                    refs[-1][(c ^ r) * size : ((c ^ r) + 1) * size] = refs[r][...].astype(dtype)

    return pl.pallas_call(
        kernel,
        in_specs=[pl.BlockSpec(memory_space=pltpu.SMEM)]
        + [pl.BlockSpec(memory_space=pltpu.VMEM)] * len(blocks),
        out_specs=pl.BlockSpec(memory_space=pltpu.VMEM),
        out_shape=jax.ShapeDtypeStruct((size * len(blocks), width), dtype),
        compiler_params=pltpu.CompilerParams(vmem_limit_bytes=32 * 2**20),
        name="join_rows",
    )(own, *blocks)


def solution(mesh):
    n_seq, n_ctx = mesh.shape["seq"], mesh.shape["ctx"]
    per_device = -(-HEADS // n_ctx)
    share = per_device * HEAD_DIM
    padded = share * n_ctx
    half = n_seq // 2
    cycle = list(range(0, n_seq, 2)) + list(range(1, n_seq, 2))[::-1]
    ring_right = [(cycle[p], cycle[(p + 1) % n_seq]) for p in range(n_seq)]
    ring_left = [(cycle[p], cycle[(p - 1) % n_seq]) for p in range(n_seq)]
    steps_right, steps_left = n_seq // 2, (n_seq - 1) // 2
    sizes = [1, per_device - 3, 1, 1] if per_device > 3 else [1] * per_device
    groups = [(sum(sizes[:g]), size) for g, size in enumerate(sizes)]

    def swap(value, distance):
        return lax.ppermute(value, "ctx", [(c, c ^ distance) for c in range(n_ctx)])

    def go_right(value):
        return lax.ppermute(value, "seq", ring_right)

    def go_left(value):
        return lax.ppermute(value, "seq", ring_left)

    def ctx_gather(value):
        blocks = [value]
        for r in range(1, n_ctx):
            blocks.append(swap(blocks[r - 1], 1) if r % 2 else swap(value, r))
        return blocks

    def with_neighbours(evens):
        return [block for even in evens for block in (even, swap(even, 1))]

    def ctx_exchange(blocks):
        return [blocks[0]] + [swap(blocks[r], r) for r in range(1, n_ctx)]

    def ctx_reduce(parts):
        total = None
        for r in range(n_ctx - 2, -1, -2):
            both = parts[r].astype(f32) + swap(parts[r + 1], 1).astype(f32)
            if r:
                both = swap(both.astype(bf16), r).astype(f32)
            total = both if total is None else total + both
        return total

    def in_order(blocks, own):
        size = blocks[0].shape[0]
        whole = jnp.zeros((size * n_ctx, *blocks[0].shape[1:]), blocks[0].dtype)
        for r, piece in enumerate(blocks):
            whole = lax.dynamic_update_slice_in_dim(whole, piece, (own ^ r) * size, 0)
        return whole

    def column_plans(width, column):
        take, give = [], []
        for c in range(n_ctx):
            moves = []
            for third in range(3):
                first, last = c * share, min((c + 1) * share, width)
                place = third * width + first
                while place < third * width + last:
                    shard = place // column
                    stop = min((shard + 1) * column, third * width + last)
                    to = third * share + place - third * width - first
                    moves.append((0, to, shard ^ c, place - shard * column, stop - place))
                    place = stop
            take.append(moves)
        for c in range(n_ctx):
            moves = []
            for d in range(n_ctx):
                for _, at, shard, start, count in take[d]:
                    if shard ^ d == c:
                        moves.append((0, start, c ^ d, at, count))
            give.append(moves)
        return take, give

    def body(
        tokens,
        segments,
        cotangent,
        gain_one,
        shift_one,
        w_qkv,
        bias_q,
        bias_v,
        w_out,
        bias_out,
        gain_two,
        shift_two,
        w_up,
        bias_up,
        w_down,
        bias_down,
    ):
        rows, width = tokens.shape[1:]
        depth = w_up.shape[0]
        hidden_own = w_up.shape[1]
        hidden = hidden_own * n_ctx
        own = lax.axis_index("ctx")
        own_array = jnp.reshape(own, (1,)).astype(jnp.int32)
        seq = lax.axis_index("seq")
        spot = jnp.where(seq % 2 == 0, seq // 2, n_seq - 1 - seq // 2)

        def ring_row(step):
            p = lax.rem(spot + (n_seq + step), n_seq)
            return jnp.where(p < half, 2 * p, 2 * (n_seq - 1 - p) + 1)

        def put(wholes, pieces, step):
            row = ring_row(step)
            return [
                lax.dynamic_update_slice_in_dim(whole, piece, row * piece.shape[0], 0)
                for whole, piece in zip(wholes, pieces)
            ]

        def blank(pieces):
            return [jnp.zeros((n_seq * p.shape[0], p.shape[1]), p.dtype) for p in pieces]

        def take(part, step):
            size = part.shape[0] // n_seq
            return lax.dynamic_slice_in_dim(part, ring_row(step) * size, size, 0)

        def step_right_left(step, right, left):
            return go_right(right), go_left(left) if step <= steps_left else None

        def pick(parts, step):
            pieces = [take(part, step).reshape(-1, parts[-1].shape[1]) for part in parts]
            return pieces[0] if len(pieces) == 1 else jnp.concatenate(pieces)

        def reduce_go(step, right, left):
            return go_right(right), go_left(left) if step > steps_right - steps_left else left

        def reduce_add(parts, step, right, left):
            if step > 1:
                right = (right.astype(f32) + pick(parts, step - 1).astype(f32)).astype(bf16)
            rest = step - (steps_right - steps_left)
            if rest > 1:
                left = (left.astype(f32) + pick(parts, 1 - rest).astype(f32)).astype(bf16)
            return right, left

        def reduce_step(parts, step, right, left):
            return reduce_add(parts, step, *reduce_go(step, right, left))

        def reduce_start(parts):
            return pick(parts, steps_right), pick(parts, -steps_left)

        def reduce_end(parts, right, left):
            return right.astype(f32) + left.astype(f32) + pick(parts, 0).astype(f32)

        def all_sum(value, beside):
            beside, stage = list(beside), 0
            for axis in ("ctx", "seq"):
                size, r = mesh.shape[axis], 1
                while r < size:
                    hops = [r, 2 * r, 3 * r] if 2 * r < size else [r]
                    others = [
                        lax.ppermute(value, axis, [(d, d ^ hop) for d in range(size)])
                        for hop in hops
                    ]
                    if stage < len(beside):
                        others[0], beside[stage] = lax.optimization_barrier(
                            (others[0], beside[stage])
                        )
                    value = value + others[0]
                    if len(hops) > 1:
                        value = value + (others[1] + others[2])
                    r, stage = r * (len(hops) + 1), stage + 1
            return value, beside

        inputs = tokens[0].astype(f32)
        upstream_low = cotangent[0]
        upstream = upstream_low.astype(f32)
        take_plan, give_plan = column_plans(width, w_qkv.shape[1])

        w_qkv_blocks = ctx_gather(w_qkv)
        normed_one, norm_back_one = jax.vjp(layer_norm, inputs, gain_one, shift_one)
        normed_one_low = normed_one.astype(bf16)
        normed_one_blocks = ctx_gather(normed_one_low)
        out_column = w_out.shape[1]
        aligned = -(-out_column // 128) * 128
        first_plan = [
            [(0, 0, n_ctx, 0, out_column)]
            + [(0, aligned + to, slot, at, count) for _, to, slot, at, count in moves]
            for moves in take_plan
        ]
        (w_first_rows,) = move_columns(
            own_array, [*w_qkv_blocks, w_out], [aligned + 3 * share], first_plan, bf16
        )
        wholes = put(blank([w_first_rows]), [w_first_rows], 0)
        right = left = w_first_rows
        for step in range(1, steps_right + 1):
            right, left = step_right_left(step, right, left)
            wholes = put(wholes, [right], -step)
            if left is not None:
                wholes = put(wholes, [left], step)
        w_qkv_own, w_out_columns = wholes[0][:, aligned:], wholes[0][:, :aligned]
        last = right

        upstream_evens = [upstream_low] + [
            swap(after(upstream_low, normed_one_blocks[-2]), r) for r in range(2, n_ctx, 2)
        ]
        w_out_evens = [w_out_columns] + [
            swap(after(w_out_columns, upstream_evens[-1]), r) for r in range(2, n_ctx, 2)
        ]
        normed_one_all = jnp.concatenate(normed_one_blocks)
        segment_all = jnp.concatenate(ctx_gather(segments[0]))
        start = jnp.zeros_like(segment_all)
        for number in range(1, 5):
            count = jnp.sum((segment_all < number).astype(jnp.int32))
            start = jnp.where(segment_all == number, count, start)
        start = start[None]

        piece, column = w_down.shape[0] // n_ctx, w_down.shape[1]
        w_down_pieces = w_down.reshape(n_ctx, piece, column)
        w_down_pieces = ctx_exchange(
            [lax.dynamic_index_in_dim(w_down_pieces, own ^ r, 0, False) for r in range(n_ctx)]
        )
        join_plan = [[(0, (c ^ r) * column, r, 0, column) for r in range(n_ctx)] for c in range(n_ctx)]
        (w_down_rows,) = move_columns(own_array, w_down_pieces, [width], join_plan, bf16)
        spread = [(b, (b % n_seq) * n_ctx + b // n_seq) for b in range(n_seq * n_ctx)]
        w_down_rows = lax.ppermute(after(w_down_rows, w_first_rows), ("seq", "ctx"), spread)
        w_mlp_rows = jnp.concatenate([w_up.reshape(-1, width), w_down_rows])

        def cut_mlp(block):
            upper, lower = jnp.split(block, 2)
            return upper.reshape(depth, hidden_own), lower

        bias_qkv = jnp.concatenate(
            [
                lax.dynamic_slice_in_dim(jnp.pad(bias, (0, padded - width)), own * share, share)
                for bias in (bias_q, jnp.zeros_like(bias_q), bias_v)
            ]
        )
        qkv = (mm(w_qkv_own, normed_one_all, (((0,), (1,)), ((), ()))) + bias_qkv[:, None]).astype(
            bf16
        )
        qkv = qkv.reshape(3, share, -1)
        wholes = put(blank(cut_mlp(w_mlp_rows)), cut_mlp(w_mlp_rows), 0)
        right = left = after(w_mlp_rows, last)
        outs, logs, arrived, step = [], [], [], 0
        for first, count in groups:
            if step < 1:
                step += 1
                right, left = step_right_left(step, right, left)
            elif left is not None and step < steps_right:
                qkv, right, left = lax.optimization_barrier((qkv, right, left))
                if step == 1:
                    qkv, *upstream_evens = lax.optimization_barrier((qkv, *upstream_evens))
                elif step == 2:
                    qkv, *w_out_evens = lax.optimization_barrier((qkv, *w_out_evens))
                wholes = put(wholes, cut_mlp(right), -step)
                if left is not None:
                    wholes = put(wholes, cut_mlp(left), step)
                step += 1
                right, left = step_right_left(step, right, left)
            out, log = attend(own_array, start, qkv, rows, first, count)
            outs.append(out)
            logs.append(log)
            if first + count == per_device or len(outs) == len(groups) - 1:
                sent = outs[-1:] if arrived else outs
                arrived.append(
                    ctx_exchange([jnp.concatenate([o[r] for o in sent]) for r in range(n_ctx)])
                )
        join_plan = [
            [(0, (c ^ r) * out_column, r, 0, out_column) for r in range(n_ctx)] for c in range(n_ctx)
        ]
        (w_out_all,) = move_columns(
            own_array, with_neighbours(w_out_evens), [width], join_plan, bf16
        )
        upstream_blocks = with_neighbours(upstream_evens)
        attended = in_order(
            [jnp.concatenate([part[r] for part in arrived]) for r in range(n_ctx)], own
        )[:width]
        attended, right = lax.optimization_barrier((attended, right))
        wholes = put(wholes, cut_mlp(right), -step)
        if left is not None:
            wholes = put(wholes, cut_mlp(left), step)
        middle = inputs + mm(attended, w_out_all, TN) + bias_out
        normed_two, norm_back_two = jax.vjp(layer_norm, middle, gain_two, shift_two)
        normed_two_low = normed_two.astype(bf16)
        while step < steps_right:
            step += 1
            if step == steps_right:
                right = after(right, normed_two_low)
            right, left = step_right_left(step, right, left)
            wholes = put(wholes, cut_mlp(right), -step)
            if left is not None:
                wholes = put(wholes, cut_mlp(left), step)
        w_up_own, w_down_own = wholes

        bias_up_own = lax.dynamic_slice_in_dim(bias_up, own * hidden_own, hidden_own)

        def feed(normed, grad):
            pre = mm(normed, w_up_own) + bias_up_own
            cumulative = 0.5 * (1.0 + lax.erf(pre * 0.5**0.5))
            activated = (pre * cumulative).astype(bf16)
            slope = cumulative + pre * jnp.exp(-0.5 * pre * pre) * (0.5 / jnp.pi) ** 0.5
            grad_pre = (mm(grad, w_down_own, NT) * slope).astype(bf16)
            return activated, grad_pre, mm(grad_pre, w_up_own, NT).astype(bf16)

        near = n_ctx // 2
        evens = [normed_two_low] + [swap(normed_two_low, r) for r in range(2, n_ctx, 2)]
        normed_near = with_neighbours(evens[: near // 2])
        normed_near = jnp.concatenate(normed_near)
        upstream_near = jnp.concatenate(upstream_blocks[:near])
        act_near, grad_pre_near, grad_norm_near = feed(normed_near, upstream_near)
        act_near, grad_pre_near, grad_norm_near, *evens = lax.optimization_barrier(
            (act_near, grad_pre_near, grad_norm_near, *evens)
        )
        normed_far = with_neighbours(evens[near // 2 :])
        normed_far = jnp.concatenate(normed_far)
        upstream_far = jnp.concatenate(upstream_blocks[near:])
        act_far, grad_pre_far, grad_norm_far = feed(normed_far, upstream_far)
        far_parts = jnp.split(grad_norm_far, near)
        far_sums = [
            (far_parts[r] + swap(far_parts[r + 1], 1)).astype(bf16) for r in range(0, near, 2)
        ]
        near_parts = jnp.split(grad_norm_near, near)
        near_sums = [
            near_parts[r].astype(f32) + swap(near_parts[r + 1], 1).astype(f32)
            for r in range(0, near, 2)
        ]
        act_near, act_far, grad_pre_near, grad_pre_far, *far_sums = lax.optimization_barrier(
            (act_near, act_far, grad_pre_near, grad_pre_far, *far_sums)
        )
        grad_norm_two = near_sums[0]
        for r in range(2, n_ctx, 2):
            part = near_sums[r // 2].astype(bf16) if r < near else far_sums[(r - near) // 2]
            grad_norm_two = grad_norm_two + swap(part, r).astype(f32)
        part_w_down = (mm(act_near, upstream_near, TN) + mm(act_far, upstream_far, TN)).astype(bf16)
        part_w_up = (mm(normed_near, grad_pre_near, TN) + mm(normed_far, grad_pre_far, TN)).astype(
            bf16
        )
        mlp_out_parts = [
            part
            for act in (act_near, act_far)
            for part in jnp.split(mm(act, w_down_own).astype(bf16), near)
        ]
        mlp_parts = [part_w_up, part_w_down]
        mlp_step = steps_right
        right, left = reduce_start(mlp_parts)
        right, left = reduce_go(mlp_step, right, left)
        grad_norm_two, *mlp_out_parts = lax.optimization_barrier((grad_norm_two, *mlp_out_parts))
        grad_middle_part, grad_gain_two, grad_shift_two = norm_back_two(grad_norm_two)
        grad_middle = upstream + grad_middle_part

        grad_branch = grad_middle.astype(bf16)
        grad_attended = mm(w_out_all, grad_branch, NT).astype(bf16)
        grad_attended = jnp.pad(grad_attended, ((0, padded - width), (0, 0)))
        grad_attended = grad_attended.reshape(n_ctx, share, -1)
        grad_attended = [
            lax.dynamic_index_in_dim(grad_attended, own ^ r, 0, False) for r in range(n_ctx)
        ]

        grad_attended, right, left = lax.optimization_barrier((grad_attended, right, left))
        right, left = reduce_add(mlp_parts, mlp_step, right, left)
        grad_owns = []
        for first, last in ((0, groups[0][1]), (groups[0][1], per_device)):
            if last > first:
                span = slice(first * HEAD_DIM, last * HEAD_DIM)
                grad_owns.append(
                    (first, jnp.stack(ctx_exchange([part[span] for part in grad_attended])))
                )
        mlp_sums = [
            mlp_out_parts[r].astype(f32) + swap(mlp_out_parts[r + 1], 1).astype(f32)
            for r in range(0, n_ctx, 2)
        ]
        mlp_far = [swap(mlp_sums[r // 2].astype(bf16), r) for r in range(2, n_ctx, 2)]
        grad_bias_up_own = jnp.sum(grad_pre_near.astype(f32), axis=0) + jnp.sum(
            grad_pre_far.astype(f32), axis=0
        )
        early = jnp.concatenate(
            [
                jnp.sum(upstream, axis=0),
                grad_gain_two,
                grad_shift_two,
                jnp.sum(grad_branch.astype(f32), axis=0),
                lax.dynamic_update_slice_in_dim(
                    jnp.zeros((hidden,), f32), grad_bias_up_own, own * hidden_own, 0
                ),
            ]
        )

        part_w_out = mm(attended, grad_branch).astype(bf16)
        back = None
        for g, ((first, count), out, log) in enumerate(zip(groups, outs, logs)):
            grad_first, grad_own = grad_owns[min(g, 1)]
            if g and mlp_step > 1:
                mlp_step -= 1
                right, left = reduce_step(mlp_parts, mlp_step, right, left)
                grad_own, right, left = lax.optimization_barrier((grad_own, right, left))
            if g == 1:
                grad_own, *mlp_sums = lax.optimization_barrier((grad_own, *mlp_sums))
                mlp_far = [swap(mlp_sums[r // 2].astype(bf16), r) for r in range(2, n_ctx, 2)]
            if g == 2:
                grad_own, *mlp_far = lax.optimization_barrier((grad_own, *mlp_far))
            back = attend_back(
                own_array, start, qkv, out, grad_own, log, rows, first, count, back, grad_first
            )
            if g == min(1, len(groups) - 1):
                part_plan = [
                    [(r, 0, 0, (c ^ r) * out_column, out_column) for r in range(n_ctx)]
                    for c in range(n_ctx)
                ]
                part_w_out = ctx_reduce(
                    move_columns(
                        own_array,
                        [after(part_w_out, back)],
                        [aligned] * n_ctx,
                        part_plan,
                        bf16,
                    )
                ).astype(bf16)
        while mlp_step > 1:
            mlp_step -= 1
            right, left = reduce_step(mlp_parts, mlp_step, right, left)
        grad_mlp_rows = reduce_end(mlp_parts, right, left)
        grad_w_up, grad_w_down_rows = jnp.split(grad_mlp_rows, 2)
        grad_w_up = grad_w_up.reshape(depth, hidden_own)
        back, part_w_out, early = lax.optimization_barrier((back, part_w_out, early))
        mlp_out = mlp_sums[0]
        for far in mlp_far:
            mlp_out = mlp_out + far.astype(f32)

        grad_proj = back.reshape(3 * share, -1)
        far_grad = grad_proj[:, near * rows :]
        far_parts = jnp.split(
            mm(far_grad, w_qkv_own, (((0,), (1,)), ((), ()))).astype(bf16), near
        )
        far_sums = [
            (far_parts[r] + swap(far_parts[r + 1], 1)).astype(bf16) for r in range(0, near, 2)
        ]
        grad_proj, grad_w_down_rows, *far_sums = lax.optimization_barrier(
            (grad_proj, grad_w_down_rows, *far_sums)
        )
        part_w_qkv = mm(normed_one_all, grad_proj, (((0,), (1,)), ((), ()))).astype(bf16)
        last_parts = [jnp.concatenate([part_w_out, part_w_qkv], axis=1)]
        right, left = reduce_start(last_parts)
        grad_proj, right, left = lax.optimization_barrier((grad_proj, right, left))
        near_parts = jnp.split(
            mm(grad_proj[:, : near * rows], w_qkv_own, (((0,), (1,)), ((), ()))).astype(bf16), near
        )
        near_sums = [
            near_parts[r].astype(f32) + swap(near_parts[r + 1], 1).astype(f32)
            for r in range(0, near, 2)
        ]
        grad_norm_one = near_sums[0]
        for r in range(2, n_ctx, 2):
            part = near_sums[r // 2].astype(bf16) if r < near else far_sums[(r - near) // 2]
            grad_norm_one = grad_norm_one + swap(part, r).astype(f32)

        for step in range(steps_right, 0, -1):
            right, left = reduce_step(last_parts, step, right, left)
            if step == steps_right - 1:
                output = (middle + mlp_out + bias_down).astype(bf16)
                grad_norm_one, right, left, output = lax.optimization_barrier(
                    (grad_norm_one, right, left, output)
                )
        last_rows = reduce_end(last_parts, right, left)
        grad_w_out = last_rows[:, :out_column]
        grad_w_qkv_rows = last_rows[:, aligned:].astype(bf16)
        (grad_w_qkv,) = move_columns(
            own_array, ctx_gather(grad_w_qkv_rows), [w_qkv.shape[1]], give_plan, f32
        )

        gathered = [(b, a) for a, b in spread]
        grad_w_down_rows = lax.ppermute(grad_w_down_rows.astype(bf16), ("seq", "ctx"), gathered)
        column = w_down.shape[1]
        part_plan = [[(r, 0, 0, (c ^ r) * column, column) for r in range(n_ctx)] for c in range(n_ctx)]
        grad_w_down_pieces = ctx_exchange(
            move_columns(
                own_array, [after(grad_w_down_rows, grad_norm_one)], [column] * n_ctx, part_plan, bf16
            )
        )
        grad_w_down = join_rows(own_array, grad_w_down_pieces, f32)

        grad_input_part, grad_gain_one, grad_shift_one = norm_back_one(grad_norm_one)
        grad_tokens = grad_middle + grad_input_part
        grad_bias_qkv = jnp.sum(back.astype(f32), axis=2)
        sums, (grad_tokens, grad_w_down) = all_sum(
            jnp.concatenate(
                [grad_gain_one, grad_shift_one]
                + [
                    lax.dynamic_update_slice_in_dim(
                        jnp.zeros((padded,), f32), grad_bias_qkv[g], own * share, 0
                    )[:width]
                    for g in (0, 2)
                ]
                + [early]
            ),
            [grad_tokens, grad_w_down],
        )
        (
            grad_gain_one,
            grad_shift_one,
            grad_bias_q,
            grad_bias_v,
            grad_bias_down,
            grad_gain_two,
            grad_shift_two,
            grad_bias_out,
        ) = (sums[g * width : (g + 1) * width] for g in range(8))
        grad_bias_up = sums[8 * width :]
        return (
            output[None],
            grad_tokens[None],
            grad_gain_one,
            grad_shift_one,
            grad_w_qkv,
            grad_bias_q,
            grad_bias_v,
            grad_w_out,
            grad_bias_out,
            grad_gain_two,
            grad_shift_two,
            grad_w_up,
            grad_bias_up,
            grad_w_down,
            grad_bias_down,
        )

    block = P("seq", "ctx", None)
    split = P("seq", "ctx")
    return jax.shard_map(
        body,
        mesh=mesh,
        in_specs=(
            block,
            split,
            block,
            P(),
            P(),
            split,
            P(),
            P(),
            split,
            P(),
            P(),
            P(),
            split,
            P(),
            split,
            P(),
        ),
        out_specs=(
            block,
            block,
            P(),
            P(),
            split,
            P(),
            P(),
            split,
            P(),
            P(),
            P(),
            split,
            P(),
            split,
            P(),
        ),
        check_vma=False,
    )
```

```python
import functools

import jax
import jax.numpy as jnp
from jax import lax
from jax.experimental import pallas as pl
from jax.experimental.pallas import tpu as pltpu
from jax.sharding import PartitionSpec as P

HEADS = 17
HEAD_DIM = 64

eps = 1e-05
neg_big = -1e30
f32 = jnp.float32
bf16 = jnp.bfloat16

NN = (((1,), (0,)), ((), ()))
NT = (((1,), (1,)), ((), ()))
TN = (((0,), (0,)), ((), ()))


def mm(left, right, dims=NN):
    return lax.dot_general(left, right, dims, preferred_element_type=f32)


def layer_norm(values, norm_gain, norm_shift):
    average = jnp.mean(values, axis=-1, keepdims=True)
    centred = values - average
    variance = jnp.mean(centred * centred, axis=-1, keepdims=True)
    return centred * lax.rsqrt(variance + eps) * norm_gain + norm_shift


def after(value, *earlier):
    return lax.optimization_barrier((value, *earlier))[0]


def allowed_tile(start, i, j, block):
    key_pos = j * block + lax.broadcasted_iota(jnp.int32, (block, block), 0)
    allowed = key_pos >= start
    if i == j:
        query_pos = i * block + lax.broadcasted_iota(jnp.int32, (block, block), 1)
        allowed = allowed & (key_pos <= query_pos)
    return allowed


def attend_kernel(block, blocks, own_ref, start_ref, qkv_ref, out_ref, log_ref):
    slots = [own_ref[0] ^ i for i in range(blocks)]
    cols = [pl.ds(pl.multiple_of(slot * block, block), block) for slot in slots]
    scale = jnp.asarray(HEAD_DIM ** (-0.5), bf16)
    for i in range(blocks):
        query = qkv_ref[0, :, cols[i]] * scale
        start = start_ref[:, cols[i]]
        scores = []
        for j in range(i + 1):
            score = mm(qkv_ref[1, :, cols[j]], query, TN)
            scores.append(jnp.where(allowed_tile(start, i, j, block), score, neg_big))
        top = functools.reduce(
            jnp.maximum, [jnp.max(score, axis=0, keepdims=True) for score in scores]
        )
        total, sums = jnp.zeros_like(top), None
        for j in range(i + 1):
            power = jnp.exp(scores[j] - top)
            total = total + jnp.sum(power, axis=0, keepdims=True)
            part = mm(qkv_ref[2, :, cols[j]], power.astype(bf16))
            sums = part if sums is None else sums + part
        out_ref[slots[i]] = (sums / total).astype(bf16)
        log_ref[0, :, cols[i]] = top + jnp.log(total)


def attend_back_kernel(
    block, blocks, own_ref, start_ref, qkv_ref, out_ref, grad_ref, log_ref, *rest
):
    back_ref, query_sum = rest[-2:]
    slots = [own_ref[0] ^ i for i in range(blocks)]
    cols = [pl.ds(pl.multiple_of(slot * block, block), block) for slot in slots]
    scale = jnp.asarray(HEAD_DIM ** (-0.5), bf16)
    dots = [
        jnp.sum(out_ref[slot].astype(f32) * grad_ref[slot].astype(f32), axis=0, keepdims=True)
        for slot in slots
    ]
    for j in range(blocks):
        key = qkv_ref[1, :, cols[j]]
        value = qkv_ref[2, :, cols[j]]
        key_sum = value_sum = None
        for i in range(j, blocks):
            query = qkv_ref[0, :, cols[i]] * scale
            grad = grad_ref[slots[i]]
            score = mm(key, query, TN)
            allowed = allowed_tile(start_ref[:, cols[i]], i, j, block)
            soft = jnp.where(allowed, jnp.exp(score - log_ref[0, :, cols[i]]), 0.0)
            back = (soft * (mm(value, grad, TN) - dots[i])).astype(bf16)
            value_part = mm(grad, soft.astype(bf16), NT)
            key_part = mm(query, back, NT)
            value_sum = value_part if value_sum is None else value_sum + value_part
            key_sum = key_part if key_sum is None else key_sum + key_part
            if j == 0:
                query_sum[i] = mm(key, back)
            else:
                query_sum[i] += mm(key, back)
        back_ref[1, :, cols[j]] = key_sum.astype(bf16)
        back_ref[2, :, cols[j]] = value_sum.astype(bf16)
    for i in range(blocks):
        back_ref[0, :, cols[i]] = (query_sum[i] * HEAD_DIM ** (-0.5)).astype(bf16)


def attend(own, start, qkv, block, first, count):
    _, width, length = qkv.shape
    blocks = length // block
    pairs = count * block * block * blocks * (blocks + 1) // 2
    return pl.pallas_call(
        functools.partial(attend_kernel, block, blocks),
        grid_spec=pltpu.PrefetchScalarGridSpec(
            num_scalar_prefetch=1,
            grid=(count,),
            in_specs=[
                pl.BlockSpec((1, length), lambda h, own: (0, 0)),
                pl.BlockSpec((3, HEAD_DIM, length), lambda h, own: (0, first + h, 0)),
            ],
            out_specs=[
                pl.BlockSpec((blocks, HEAD_DIM, block), lambda h, own: (0, h, 0)),
                pl.BlockSpec((1, 1, length), lambda h, own: (h, 0, 0)),
            ],
        ),
        out_shape=[
            jax.ShapeDtypeStruct((blocks, count * HEAD_DIM, block), bf16),
            jax.ShapeDtypeStruct((count, 1, length), f32),
        ],
        compiler_params=pltpu.CompilerParams(vmem_limit_bytes=24 * 2**20),
        cost_estimate=pl.CostEstimate(
            flops=pairs * 4 * 256 * 2,
            bytes_accessed=count * HEAD_DIM * length * 8,
            transcendentals=pairs,
        ),
        name="attend",
    )(own, start, qkv)


def attend_back(own, start, qkv, out, grad, log, block, first, count, held, grad_first):
    _, width, length = qkv.shape
    blocks = length // block
    pairs = count * block * block * blocks * (blocks + 1) // 2
    tile = pl.BlockSpec((3, HEAD_DIM, length), lambda h, own: (0, first + h, 0))
    side = pl.BlockSpec((blocks, HEAD_DIM, block), lambda h, own: (0, h, 0))
    in_specs = [
        pl.BlockSpec((1, length), lambda h, own: (0, 0)),
        tile,
        side,
        pl.BlockSpec((blocks, HEAD_DIM, block), lambda h, own: (0, first - grad_first + h, 0)),
        pl.BlockSpec((1, 1, length), lambda h, own: (h, 0, 0)),
    ]
    operands = (own, start, qkv, out, grad, log)
    aliases = {}
    if held is not None:
        in_specs.append(pl.BlockSpec(memory_space=pl.ANY))
        operands = (*operands, held)
        aliases = {len(operands) - 1: 0}
    return pl.pallas_call(
        functools.partial(attend_back_kernel, block, blocks),
        grid_spec=pltpu.PrefetchScalarGridSpec(
            num_scalar_prefetch=1,
            grid=(count,),
            in_specs=in_specs,
            out_specs=tile,
            scratch_shapes=[pltpu.VMEM((blocks, HEAD_DIM, block), f32)],
        ),
        out_shape=jax.ShapeDtypeStruct(qkv.shape, bf16),
        input_output_aliases=aliases,
        compiler_params=pltpu.CompilerParams(vmem_limit_bytes=24 * 2**20),
        cost_estimate=pl.CostEstimate(
            flops=pairs * 8 * 256 * 2,
            bytes_accessed=count * HEAD_DIM * length * 18,
            transcendentals=pairs,
        ),
        name="attend_back",
    )(*operands)


def move_columns(own, sources, widths, plan, dtype):
    rows = sources[0].shape[0]

    def kernel(own_ref, *refs):
        source_refs, target_refs = refs[: len(sources)], refs[len(sources) :]
        for c, moves in enumerate(plan):

            @pl.when(own_ref[0] == c)
            def _():
                for t, (ref, width) in enumerate(zip(target_refs, widths)):
                    covered = sum(move[4] for move in moves if move[0] == t)
                    if covered < width:
                        ref[...] = jnp.zeros_like(ref)
                for t, to, s, start, count in moves:
                    piece = source_refs[s][:, start : start + count]
                    target_refs[t][:, to : to + count] = piece.astype(dtype)

    return pl.pallas_call(
        kernel,
        in_specs=[pl.BlockSpec(memory_space=pltpu.SMEM)]
        + [pl.BlockSpec(memory_space=pltpu.VMEM)] * len(sources),
        out_specs=[pl.BlockSpec(memory_space=pltpu.VMEM)] * len(widths),
        out_shape=[jax.ShapeDtypeStruct((rows, width), dtype) for width in widths],
        compiler_params=pltpu.CompilerParams(vmem_limit_bytes=32 * 2**20),
        name="move_columns",
    )(own, *sources)


def join_rows(own, blocks, dtype):
    size, width = blocks[0].shape

    def kernel(own_ref, *refs):
        for c in range(len(blocks)):

            @pl.when(own_ref[0] == c)
            def _():
                for r in range(len(blocks)):
                    refs[-1][(c ^ r) * size : ((c ^ r) + 1) * size] = refs[r][...].astype(dtype)

    return pl.pallas_call(
        kernel,
        in_specs=[pl.BlockSpec(memory_space=pltpu.SMEM)]
        + [pl.BlockSpec(memory_space=pltpu.VMEM)] * len(blocks),
        out_specs=pl.BlockSpec(memory_space=pltpu.VMEM),
        out_shape=jax.ShapeDtypeStruct((size * len(blocks), width), dtype),
        compiler_params=pltpu.CompilerParams(vmem_limit_bytes=32 * 2**20),
        name="join_rows",
    )(own, *blocks)


def solution(mesh):
    n_seq, n_ctx = mesh.shape["seq"], mesh.shape["ctx"]
    per_device = -(-HEADS // n_ctx)
    share = per_device * HEAD_DIM
    padded = share * n_ctx
    half = n_seq // 2
    cycle = list(range(0, n_seq, 2)) + list(range(1, n_seq, 2))[::-1]
    ring_right = [(cycle[p], cycle[(p + 1) % n_seq]) for p in range(n_seq)]
    ring_left = [(cycle[p], cycle[(p - 1) % n_seq]) for p in range(n_seq)]
    steps_right, steps_left = n_seq // 2, (n_seq - 1) // 2
    sizes = [1, per_device - 3, 1, 1] if per_device > 3 else [1] * per_device
    groups = [(sum(sizes[:g]), size) for g, size in enumerate(sizes)]

    def swap(value, distance):
        return lax.ppermute(value, "ctx", [(c, c ^ distance) for c in range(n_ctx)])

    def go_right(value):
        return lax.ppermute(value, "seq", ring_right)

    def go_left(value):
        return lax.ppermute(value, "seq", ring_left)

    def ctx_gather(value):
        blocks = [value]
        for r in range(1, n_ctx):
            blocks.append(swap(blocks[r - 1], 1) if r % 2 else swap(value, r))
        return blocks

    def with_neighbours(evens):
        return [block for even in evens for block in (even, swap(even, 1))]

    def ctx_exchange(blocks):
        return [blocks[0]] + [swap(blocks[r], r) for r in range(1, n_ctx)]

    def ctx_reduce(parts):
        total = None
        for r in range(n_ctx - 2, -1, -2):
            both = parts[r].astype(f32) + swap(parts[r + 1], 1).astype(f32)
            if r:
                both = swap(both.astype(bf16), r).astype(f32)
            total = both if total is None else total + both
        return total

    def in_order(blocks, own):
        size = blocks[0].shape[0]
        whole = jnp.zeros((size * n_ctx, *blocks[0].shape[1:]), blocks[0].dtype)
        for r, piece in enumerate(blocks):
            whole = lax.dynamic_update_slice_in_dim(whole, piece, (own ^ r) * size, 0)
        return whole

    def column_plans(width, column):
        take, give = [], []
        for c in range(n_ctx):
            moves = []
            for third in range(3):
                first, last = c * share, min((c + 1) * share, width)
                place = third * width + first
                while place < third * width + last:
                    shard = place // column
                    stop = min((shard + 1) * column, third * width + last)
                    to = third * share + place - third * width - first
                    moves.append((0, to, shard ^ c, place - shard * column, stop - place))
                    place = stop
            take.append(moves)
        for c in range(n_ctx):
            moves = []
            for d in range(n_ctx):
                for _, at, shard, start, count in take[d]:
                    if shard ^ d == c:
                        moves.append((0, start, c ^ d, at, count))
            give.append(moves)
        return take, give

    def body(
        tokens,
        segments,
        cotangent,
        gain_one,
        shift_one,
        w_qkv,
        bias_q,
        bias_v,
        w_out,
        bias_out,
        gain_two,
        shift_two,
        w_up,
        bias_up,
        w_down,
        bias_down,
    ):
        rows, width = tokens.shape[1:]
        depth = w_up.shape[0]
        hidden_own = w_up.shape[1]
        hidden = hidden_own * n_ctx
        own = lax.axis_index("ctx")
        own_array = jnp.reshape(own, (1,)).astype(jnp.int32)
        seq = lax.axis_index("seq")
        spot = jnp.where(seq % 2 == 0, seq // 2, n_seq - 1 - seq // 2)

        def ring_row(step):
            p = lax.rem(spot + (n_seq + step), n_seq)
            return jnp.where(p < half, 2 * p, 2 * (n_seq - 1 - p) + 1)

        def put(wholes, pieces, step):
            row = ring_row(step)
            return [
                lax.dynamic_update_slice_in_dim(whole, piece, row * piece.shape[0], 0)
                for whole, piece in zip(wholes, pieces)
            ]

        def blank(pieces):
            return [jnp.zeros((n_seq * p.shape[0], p.shape[1]), p.dtype) for p in pieces]

        def take(part, step):
            size = part.shape[0] // n_seq
            return lax.dynamic_slice_in_dim(part, ring_row(step) * size, size, 0)

        def step_right_left(step, right, left):
            return go_right(right), go_left(left) if step <= steps_left else None

        def pick(parts, step):
            pieces = [take(part, step).reshape(-1, parts[-1].shape[1]) for part in parts]
            return pieces[0] if len(pieces) == 1 else jnp.concatenate(pieces)

        def reduce_go(step, right, left):
            return go_right(right), go_left(left) if step > steps_right - steps_left else left

        def reduce_add(parts, step, right, left):
            if step > 1:
                right = (right.astype(f32) + pick(parts, step - 1).astype(f32)).astype(bf16)
            rest = step - (steps_right - steps_left)
            if rest > 1:
                left = (left.astype(f32) + pick(parts, 1 - rest).astype(f32)).astype(bf16)
            return right, left

        def reduce_step(parts, step, right, left):
            return reduce_add(parts, step, *reduce_go(step, right, left))

        def reduce_start(parts):
            return pick(parts, steps_right), pick(parts, -steps_left)

        def reduce_end(parts, right, left):
            return right.astype(f32) + left.astype(f32) + pick(parts, 0).astype(f32)

        def all_sum(value, beside):
            beside, stage = list(beside), 0
            for axis in ("ctx", "seq"):
                size, r = mesh.shape[axis], 1
                while r < size:
                    hops = [r, 2 * r, 3 * r] if 2 * r < size else [r]
                    others = [
                        lax.ppermute(value, axis, [(d, d ^ hop) for d in range(size)])
                        for hop in hops
                    ]
                    if stage < len(beside):
                        others[0], beside[stage] = lax.optimization_barrier(
                            (others[0], beside[stage])
                        )
                    value = value + others[0]
                    if len(hops) > 1:
                        value = value + (others[1] + others[2])
                    r, stage = r * (len(hops) + 1), stage + 1
            return value, beside

        inputs = tokens[0].astype(f32)
        upstream_low = cotangent[0]
        upstream = upstream_low.astype(f32)
        take_plan, give_plan = column_plans(width, w_qkv.shape[1])

        w_qkv_blocks = ctx_gather(w_qkv)
        normed_one, norm_back_one = jax.vjp(layer_norm, inputs, gain_one, shift_one)
        normed_one_low = normed_one.astype(bf16)
        normed_one_blocks = ctx_gather(normed_one_low)
        out_column = w_out.shape[1]
        aligned = -(-out_column // 128) * 128
        first_plan = [
            [(0, 0, n_ctx, 0, out_column)]
            + [(0, aligned + to, slot, at, count) for _, to, slot, at, count in moves]
            for moves in take_plan
        ]
        (w_first_rows,) = move_columns(
            own_array, [*w_qkv_blocks, w_out], [aligned + 3 * share], first_plan, bf16
        )
        wholes = put(blank([w_first_rows]), [w_first_rows], 0)
        right = left = w_first_rows
        for step in range(1, steps_right + 1):
            right, left = step_right_left(step, right, left)
            wholes = put(wholes, [right], -step)
            if left is not None:
                wholes = put(wholes, [left], step)
        w_qkv_own, w_out_columns = wholes[0][:, aligned:], wholes[0][:, :aligned]
        last = right

        upstream_evens = [upstream_low] + [
            swap(after(upstream_low, normed_one_blocks[-2]), r) for r in range(2, n_ctx, 2)
        ]
        w_out_evens = [w_out_columns] + [
            swap(after(w_out_columns, upstream_evens[-1]), r) for r in range(2, n_ctx, 2)
        ]
        normed_one_all = jnp.concatenate(normed_one_blocks)
        segment_all = jnp.concatenate(ctx_gather(segments[0]))
        start = jnp.zeros_like(segment_all)
        for number in range(1, 5):
            count = jnp.sum((segment_all < number).astype(jnp.int32))
            start = jnp.where(segment_all == number, count, start)
        start = start[None]

        piece, column = w_down.shape[0] // n_ctx, w_down.shape[1]
        w_down_pieces = w_down.reshape(n_ctx, piece, column)
        w_down_pieces = ctx_exchange(
            [lax.dynamic_index_in_dim(w_down_pieces, own ^ r, 0, False) for r in range(n_ctx)]
        )
        join_plan = [[(0, (c ^ r) * column, r, 0, column) for r in range(n_ctx)] for c in range(n_ctx)]
        (w_down_rows,) = move_columns(own_array, w_down_pieces, [width], join_plan, bf16)
        spread = [(b, (b % n_seq) * n_ctx + b // n_seq) for b in range(n_seq * n_ctx)]
        w_down_rows = lax.ppermute(after(w_down_rows, w_first_rows), ("seq", "ctx"), spread)
        w_mlp_rows = jnp.concatenate([w_up.reshape(-1, width), w_down_rows])

        def cut_mlp(block):
            upper, lower = jnp.split(block, 2)
            return upper.reshape(depth, hidden_own), lower

        bias_qkv = jnp.concatenate(
            [
                lax.dynamic_slice_in_dim(jnp.pad(bias, (0, padded - width)), own * share, share)
                for bias in (bias_q, jnp.zeros_like(bias_q), bias_v)
            ]
        )
        qkv = (mm(w_qkv_own, normed_one_all, (((0,), (1,)), ((), ()))) + bias_qkv[:, None]).astype(
            bf16
        )
        qkv = qkv.reshape(3, share, -1)
        wholes = put(blank(cut_mlp(w_mlp_rows)), cut_mlp(w_mlp_rows), 0)
        right = left = after(w_mlp_rows, last)
        outs, logs, arrived, step = [], [], [], 0
        for first, count in groups:
            if step < 1:
                step += 1
                right, left = step_right_left(step, right, left)
            elif left is not None and step < steps_right:
                qkv, right, left = lax.optimization_barrier((qkv, right, left))
                if step == 1:
                    qkv, *upstream_evens = lax.optimization_barrier((qkv, *upstream_evens))
                elif step == 2:
                    qkv, *w_out_evens = lax.optimization_barrier((qkv, *w_out_evens))
                wholes = put(wholes, cut_mlp(right), -step)
                if left is not None:
                    wholes = put(wholes, cut_mlp(left), step)
                step += 1
                right, left = step_right_left(step, right, left)
            out, log = attend(own_array, start, qkv, rows, first, count)
            outs.append(out)
            logs.append(log)
            if first + count == per_device or len(outs) == len(groups) - 1:
                sent = outs[-1:] if arrived else outs
                arrived.append(
                    ctx_exchange([jnp.concatenate([o[r] for o in sent]) for r in range(n_ctx)])
                )
        join_plan = [
            [(0, (c ^ r) * out_column, r, 0, out_column) for r in range(n_ctx)] for c in range(n_ctx)
        ]
        (w_out_all,) = move_columns(
            own_array, with_neighbours(w_out_evens), [width], join_plan, bf16
        )
        upstream_blocks = with_neighbours(upstream_evens)
        attended = in_order(
            [jnp.concatenate([part[r] for part in arrived]) for r in range(n_ctx)], own
        )[:width]
        attended, right = lax.optimization_barrier((attended, right))
        wholes = put(wholes, cut_mlp(right), -step)
        if left is not None:
            wholes = put(wholes, cut_mlp(left), step)
        middle = inputs + mm(attended, w_out_all, TN) + bias_out
        normed_two, norm_back_two = jax.vjp(layer_norm, middle, gain_two, shift_two)
        normed_two_low = normed_two.astype(bf16)
        while step < steps_right:
            step += 1
            if step == steps_right:
                right = after(right, normed_two_low)
            right, left = step_right_left(step, right, left)
            wholes = put(wholes, cut_mlp(right), -step)
            if left is not None:
                wholes = put(wholes, cut_mlp(left), step)
        w_up_own, w_down_own = wholes

        bias_up_own = lax.dynamic_slice_in_dim(bias_up, own * hidden_own, hidden_own)

        def feed(normed, grad):
            pre = mm(normed, w_up_own) + bias_up_own
            cumulative = 0.5 * (1.0 + lax.erf(pre * 0.5**0.5))
            activated = (pre * cumulative).astype(bf16)
            slope = cumulative + pre * jnp.exp(-0.5 * pre * pre) * (0.5 / jnp.pi) ** 0.5
            grad_pre = (mm(grad, w_down_own, NT) * slope).astype(bf16)
            return activated, grad_pre, mm(grad_pre, w_up_own, NT).astype(bf16)

        near = n_ctx // 2
        evens = [normed_two_low] + [swap(normed_two_low, r) for r in range(2, n_ctx, 2)]
        normed_near = with_neighbours(evens[: near // 2])
        normed_near = jnp.concatenate(normed_near)
        upstream_near = jnp.concatenate(upstream_blocks[:near])
        act_near, grad_pre_near, grad_norm_near = feed(normed_near, upstream_near)
        act_near, grad_pre_near, grad_norm_near, *evens = lax.optimization_barrier(
            (act_near, grad_pre_near, grad_norm_near, *evens)
        )
        normed_far = with_neighbours(evens[near // 2 :])
        normed_far = jnp.concatenate(normed_far)
        upstream_far = jnp.concatenate(upstream_blocks[near:])
        act_far, grad_pre_far, grad_norm_far = feed(normed_far, upstream_far)
        far_parts = jnp.split(grad_norm_far, near)
        far_sums = [
            (far_parts[r] + swap(far_parts[r + 1], 1)).astype(bf16) for r in range(0, near, 2)
        ]
        near_parts = jnp.split(grad_norm_near, near)
        near_sums = [
            near_parts[r].astype(f32) + swap(near_parts[r + 1], 1).astype(f32)
            for r in range(0, near, 2)
        ]
        act_near, act_far, grad_pre_near, grad_pre_far, *far_sums = lax.optimization_barrier(
            (act_near, act_far, grad_pre_near, grad_pre_far, *far_sums)
        )
        grad_norm_two = near_sums[0]
        for r in range(2, n_ctx, 2):
            part = near_sums[r // 2].astype(bf16) if r < near else far_sums[(r - near) // 2]
            grad_norm_two = grad_norm_two + swap(part, r).astype(f32)
        part_w_down = (mm(act_near, upstream_near, TN) + mm(act_far, upstream_far, TN)).astype(bf16)
        part_w_up = (mm(normed_near, grad_pre_near, TN) + mm(normed_far, grad_pre_far, TN)).astype(
            bf16
        )
        mlp_out_parts = [
            part
            for act in (act_near, act_far)
            for part in jnp.split(mm(act, w_down_own).astype(bf16), near)
        ]
        mlp_parts = [part_w_up, part_w_down]
        mlp_step = steps_right
        right, left = reduce_start(mlp_parts)
        right, left = reduce_go(mlp_step, right, left)
        grad_norm_two, *mlp_out_parts = lax.optimization_barrier((grad_norm_two, *mlp_out_parts))
        grad_middle_part, grad_gain_two, grad_shift_two = norm_back_two(grad_norm_two)
        grad_middle = upstream + grad_middle_part

        grad_branch = grad_middle.astype(bf16)
        grad_attended = mm(w_out_all, grad_branch, NT).astype(bf16)
        grad_attended = jnp.pad(grad_attended, ((0, padded - width), (0, 0)))
        grad_attended = grad_attended.reshape(n_ctx, share, -1)
        grad_attended = [
            lax.dynamic_index_in_dim(grad_attended, own ^ r, 0, False) for r in range(n_ctx)
        ]

        grad_attended, right, left = lax.optimization_barrier((grad_attended, right, left))
        right, left = reduce_add(mlp_parts, mlp_step, right, left)
        grad_owns = []
        for first, last in ((0, groups[0][1]), (groups[0][1], per_device)):
            if last > first:
                span = slice(first * HEAD_DIM, last * HEAD_DIM)
                sent = [part[span] for part in grad_attended]
                if grad_owns:
                    sent = after(sent, grad_owns[0][1])
                grad_owns.append((first, jnp.stack(ctx_exchange(sent))))
        mlp_sums = [
            mlp_out_parts[r].astype(f32) + swap(mlp_out_parts[r + 1], 1).astype(f32)
            for r in range(0, n_ctx, 2)
        ]
        mlp_far = [swap(mlp_sums[r // 2].astype(bf16), r) for r in range(2, n_ctx, 2)]
        grad_bias_up_own = jnp.sum(grad_pre_near.astype(f32), axis=0) + jnp.sum(
            grad_pre_far.astype(f32), axis=0
        )
        early = jnp.concatenate(
            [
                jnp.sum(upstream, axis=0),
                grad_gain_two,
                grad_shift_two,
                jnp.sum(grad_branch.astype(f32), axis=0),
                lax.dynamic_update_slice_in_dim(
                    jnp.zeros((hidden,), f32), grad_bias_up_own, own * hidden_own, 0
                ),
            ]
        )

        part_w_out = mm(attended, grad_branch).astype(bf16)
        back = None
        for g, ((first, count), out, log) in enumerate(zip(groups, outs, logs)):
            grad_first, grad_own = grad_owns[min(g, 1)]
            if g and mlp_step > 1:
                mlp_step -= 1
                right, left = reduce_step(mlp_parts, mlp_step, right, left)
                grad_own, right, left = lax.optimization_barrier((grad_own, right, left))
            if g == 1:
                grad_own, *mlp_sums = lax.optimization_barrier((grad_own, *mlp_sums))
                mlp_far = [swap(mlp_sums[r // 2].astype(bf16), r) for r in range(2, n_ctx, 2)]
            if g == 2:
                grad_own, *mlp_far = lax.optimization_barrier((grad_own, *mlp_far))
            back = attend_back(
                own_array, start, qkv, out, grad_own, log, rows, first, count, back, grad_first
            )
            if g == min(1, len(groups) - 1):
                part_plan = [
                    [(r, 0, 0, (c ^ r) * out_column, out_column) for r in range(n_ctx)]
                    for c in range(n_ctx)
                ]
                part_w_out = ctx_reduce(
                    move_columns(
                        own_array,
                        [after(part_w_out, back)],
                        [aligned] * n_ctx,
                        part_plan,
                        bf16,
                    )
                ).astype(bf16)
        while mlp_step > 1:
            mlp_step -= 1
            right, left = reduce_step(mlp_parts, mlp_step, right, left)
        grad_mlp_rows = reduce_end(mlp_parts, right, left)
        grad_w_up, grad_w_down_rows = jnp.split(grad_mlp_rows, 2)
        grad_w_up = grad_w_up.reshape(depth, hidden_own)
        back, part_w_out, early = lax.optimization_barrier((back, part_w_out, early))
        mlp_out = mlp_sums[0]
        for far in mlp_far:
            mlp_out = mlp_out + far.astype(f32)

        grad_proj = back.reshape(3 * share, -1)
        far_grad = grad_proj[:, near * rows :]
        far_parts = jnp.split(
            mm(far_grad, w_qkv_own, (((0,), (1,)), ((), ()))).astype(bf16), near
        )
        far_sums = [
            (far_parts[r] + swap(far_parts[r + 1], 1)).astype(bf16) for r in range(0, near, 2)
        ]
        grad_proj, grad_w_down_rows, *far_sums = lax.optimization_barrier(
            (grad_proj, grad_w_down_rows, *far_sums)
        )
        part_w_qkv = mm(normed_one_all, grad_proj, (((0,), (1,)), ((), ()))).astype(bf16)
        last_parts = [jnp.concatenate([part_w_out, part_w_qkv], axis=1)]
        right, left = reduce_start(last_parts)
        grad_proj, right, left = lax.optimization_barrier((grad_proj, right, left))
        near_parts = jnp.split(
            mm(grad_proj[:, : near * rows], w_qkv_own, (((0,), (1,)), ((), ()))).astype(bf16), near
        )
        near_sums = [
            near_parts[r].astype(f32) + swap(near_parts[r + 1], 1).astype(f32)
            for r in range(0, near, 2)
        ]
        grad_norm_one = near_sums[0]
        for r in range(2, n_ctx, 2):
            part = near_sums[r // 2].astype(bf16) if r < near else far_sums[(r - near) // 2]
            grad_norm_one = grad_norm_one + swap(part, r).astype(f32)

        for step in range(steps_right, 0, -1):
            right, left = reduce_step(last_parts, step, right, left)
            if step == steps_right - 1:
                output = (middle + mlp_out + bias_down).astype(bf16)
                grad_norm_one, right, left, output = lax.optimization_barrier(
                    (grad_norm_one, right, left, output)
                )
        last_rows = reduce_end(last_parts, right, left)
        grad_w_out = last_rows[:, :out_column]
        grad_w_qkv_rows = last_rows[:, aligned:].astype(bf16)
        (grad_w_qkv,) = move_columns(
            own_array, ctx_gather(grad_w_qkv_rows), [w_qkv.shape[1]], give_plan, f32
        )

        gathered = [(b, a) for a, b in spread]
        grad_w_down_rows = lax.ppermute(grad_w_down_rows.astype(bf16), ("seq", "ctx"), gathered)
        column = w_down.shape[1]
        part_plan = [[(r, 0, 0, (c ^ r) * column, column) for r in range(n_ctx)] for c in range(n_ctx)]
        grad_w_down_pieces = ctx_exchange(
            move_columns(
                own_array, [after(grad_w_down_rows, grad_norm_one)], [column] * n_ctx, part_plan, bf16
            )
        )
        grad_w_down = join_rows(own_array, grad_w_down_pieces, f32)

        grad_input_part, grad_gain_one, grad_shift_one = norm_back_one(grad_norm_one)
        grad_tokens = grad_middle + grad_input_part
        grad_bias_qkv = jnp.sum(back.astype(f32), axis=2)
        sums, (grad_tokens, grad_w_down) = all_sum(
            jnp.concatenate(
                [grad_gain_one, grad_shift_one]
                + [
                    lax.dynamic_update_slice_in_dim(
                        jnp.zeros((padded,), f32), grad_bias_qkv[g], own * share, 0
                    )[:width]
                    for g in (0, 2)
                ]
                + [early]
            ),
            [grad_tokens, grad_w_down],
        )
        (
            grad_gain_one,
            grad_shift_one,
            grad_bias_q,
            grad_bias_v,
            grad_bias_down,
            grad_gain_two,
            grad_shift_two,
            grad_bias_out,
        ) = (sums[g * width : (g + 1) * width] for g in range(8))
        grad_bias_up = sums[8 * width :]
        return (
            output[None],
            grad_tokens[None],
            grad_gain_one,
            grad_shift_one,
            grad_w_qkv,
            grad_bias_q,
            grad_bias_v,
            grad_w_out,
            grad_bias_out,
            grad_gain_two,
            grad_shift_two,
            grad_w_up,
            grad_bias_up,
            grad_w_down,
            grad_bias_down,
        )

    block = P("seq", "ctx", None)
    split = P("seq", "ctx")
    return jax.shard_map(
        body,
        mesh=mesh,
        in_specs=(
            block,
            split,
            block,
            P(),
            P(),
            split,
            P(),
            P(),
            split,
            P(),
            P(),
            P(),
            split,
            P(),
            split,
            P(),
        ),
        out_specs=(
            block,
            block,
            P(),
            P(),
            split,
            P(),
            P(),
            split,
            P(),
            P(),
            P(),
            split,
            P(),
            split,
            P(),
        ),
        check_vma=False,
    )
```
